256 devices in a mesh: ctx: 32 (over z, x_lo, core), head: 8 (over y, x_hi).
Axes of the slice: x: 4 (x_hi: 2, x_lo: 2; x = x_hi * 2 + x_lo), y: 4, z: 8, core: 2. Of those that a mesh axis runs over, the one named last changes fastest.
Arguments:
- queries: bfloat16 [8192, 8192], P('ctx', 'head'), may hold values from -6.5 to 6.5
- keys: bfloat16 [8192, 1024], P('ctx', 'head'), may hold values from -6.5 to 6.5
- values: bfloat16 [8192, 1024], P('ctx', 'head'), may hold values from -6 to 6
- doc_lengths: int32 [8], replicated, may hold values from 1 to 4096, 8192 in all
- out_weight: bfloat16 [8192, 4096], P(None, 'head'), may hold values from -0.0625 to 0.0625
Outputs:
- projected: bfloat16 [8192, 4096], P('ctx', 'head')
The draws below stay inside these ranges and needn't reach their ends.
Inputs may be any that keep to these rules, and one draw needn't show every extreme that they name: `doc_lengths`: the lengths sum to 8192; the longest document has exactly 4096 tokens.
All inputs are finite; a program needn't handle non-finite values.
Results may differ from the reference program's by a relative error of at most 0.009.
Values may be sent and summed in bfloat16 or wider, within the bound.
No kernel may reach another device: no remote copies, remote signals or barrier semaphores. Data moves between devices by JAX's collectives and lax.ppermute only.
A program may use at most 64 MiB of HBM per device.

```python
import math
import jax
import jax.numpy as jnp
import numpy as np
from jax import lax

HEAD_DIM = 128
GROUP = 8
KV_HEADS = 8
Q_HEADS = 64
D_OUT = 4096
SEQ = 8192
NDOCS = 8


def draw_queries(key, part):
    shape = (SEQ, Q_HEADS * HEAD_DIM)
    base = jnp.clip(jax.random.normal(jax.random.fold_in(key, 11), shape, jnp.float32), -4.0, 4.0)
    return base.astype(jnp.bfloat16)


def draw_keys(key, part):
    shape = (SEQ, KV_HEADS * HEAD_DIM)
    base = jnp.clip(jax.random.normal(jax.random.fold_in(key, 13), shape, jnp.float32), -4.0, 4.0)
    return base.astype(jnp.bfloat16)


def levels(rng, shape, pieces, low, largest):
    level, own = 1.0, jax.random.fold_in(rng, 6)
    for axis_at, parts in pieces:
        steps = jnp.exp(jax.random.uniform(jax.random.fold_in(own, axis_at), (parts,), jnp.float32, low / len(pieces), largest / len(pieces)))
        level = level * jnp.repeat(steps, shape[axis_at] // parts).reshape([-1 if axis == axis_at else 1 for axis in range(len(shape))])
    return level


def split_up(number_of, total, limit, skew):
    loads = [(1 << 20) // math.isqrt(grade ** skew) + 1 for grade in range(2, number_of + 1)]
    surplus, holding = total - limit - (number_of - 1), [1] * (number_of - 1)
    while surplus > 0:
        candidates = [i for i in range(number_of - 1) if holding[i] < limit]
        whole, budget = sum([loads[i] for i in candidates]), surplus
        for i in candidates:
            addition = min(limit - holding[i], max(1, budget * loads[i] // whole), surplus)
            holding[i] = holding[i] + addition
            surplus = surplus - addition
    return np.array([limit] + holding)


def ragged_sizes(own_key, amount, total, bound, skew):
    if amount == 2:
        one = jax.random.randint(own_key, (), max(1, total - bound), min(bound, total - 1) + 1)
        return jnp.stack([one, total - one])
    sizes = jnp.asarray(split_up(amount, total, bound, skew), jnp.int32)
    couples = (amount - 1) // 2
    giver, sink = sizes[1:1 + 2 * couples:2], sizes[2:2 + 2 * couples:2]
    margin = jnp.minimum(giver - 1, bound - sink)
    shifted = jax.random.randint(jax.random.fold_in(own_key, 1), (couples,), 0, 1 << 20) % (margin + 1)
    sizes = sizes.at[1:1 + 2 * couples:2].set(giver - shifted).at[2:2 + 2 * couples:2].set(sink + shifted)
    return sizes[jax.random.permutation(jax.random.fold_in(own_key, 2), amount)]


def scatter_about(rng, extent, width, bound, cuts=(), held_as=jnp.bfloat16):
    drawn = jax.random.normal(rng, extent, jnp.float32) * width
    if len(cuts) > 0:
        drawn = levels(rng, extent, cuts, -0.22, 0.18) * drawn
    return jnp.clip(drawn, min=-bound, max=bound).astype(held_as)


def setup_inputs(seed: int = 0) -> dict:
    arg_keys = jax.random.split(jax.random.key(seed), 6)
    queries = draw_queries(jax.random.fold_in(arg_keys[5], 71), 0)
    keys = draw_keys(jax.random.fold_in(arg_keys[5], 71), 0)
    values = scatter_about(arg_keys[2], (SEQ, KV_HEADS * HEAD_DIM), 1.0, 6.0, ((0, 32), (1, 8)))
    doc_lengths = ragged_sizes(arg_keys[3], NDOCS, SEQ, SEQ // 2, 2).astype(jnp.int32)
    out_weight = scatter_about(arg_keys[4], (Q_HEADS * HEAD_DIM, D_OUT), (Q_HEADS * HEAD_DIM) ** -0.5, 0.0625, ((1, 8),))
    return {"queries": queries, "keys": keys, "values": values, "doc_lengths": doc_lengths, "out_weight": out_weight}


LOW_SCORE = -1e+30

def doc_numbers(doc_ends, positions):
    return lax.optimization_barrier(jnp.sum((doc_ends[None, :] <= positions[:, None]).astype(jnp.int32), axis=1))

def reference(queries, keys, values, doc_lengths, out_weight):
    seq_len = queries.shape[0]
    groups = keys.shape[1] // HEAD_DIM
    q_block = math.gcd(seq_len, 512)
    block_count = seq_len // q_block
    doc_ends = jnp.cumsum(doc_lengths).astype(jnp.int32)
    positions = jnp.arange(seq_len, dtype=jnp.int32)
    documents = doc_numbers(doc_ends, positions)
    grouped = queries.reshape(seq_len, groups, GROUP, HEAD_DIM)
    score_scale = 1.0 / math.sqrt(HEAD_DIM)

    def one_block(index):
        group_id = index // block_count
        begin_at = index % block_count * q_block
        zero_index = jnp.zeros((), jnp.int32)
        query_tile = lax.dynamic_slice(grouped, (begin_at, group_id, zero_index, zero_index), (q_block, 1, GROUP, HEAD_DIM))[:, 0].astype(jnp.float32)
        key_tile = lax.dynamic_slice_in_dim(keys, group_id * HEAD_DIM, HEAD_DIM, 1).astype(jnp.float32)
        value_tile = lax.dynamic_slice_in_dim(values, group_id * HEAD_DIM, HEAD_DIM, 1).astype(jnp.float32)
        scores = jnp.einsum('tjd,ud->jtu', query_tile, key_tile) * score_scale
        query_pos = begin_at + jnp.arange(q_block, dtype=jnp.int32)
        query_doc = lax.dynamic_slice_in_dim(documents, begin_at, q_block)
        allowed = (positions[None, :] <= query_pos[:, None]) & (documents[None, :] == query_doc[:, None])
        scores = jnp.where(allowed[None], scores, LOW_SCORE)
        row_max = lax.optimization_barrier(jnp.max(scores, axis=-1, keepdims=True))
        exp_scores = jnp.where(allowed[None], jnp.exp(scores - row_max), 0.0)
        row_sums = lax.optimization_barrier(jnp.sum(exp_scores, axis=-1))
        rounded = lax.optimization_barrier(exp_scores.astype(jnp.bfloat16)).astype(jnp.float32)
        mixed = jnp.einsum('jtu,ud->tjd', rounded, value_tile) / jnp.transpose(row_sums)[:, :, None]
        return mixed.astype(jnp.bfloat16)
    indices = jnp.arange(groups * block_count, dtype=jnp.int32)
    stacked = lax.map(one_block, indices)
    stacked = stacked.reshape(groups, block_count, q_block, GROUP, HEAD_DIM)
    head_outs = jnp.transpose(stacked, (1, 2, 0, 3, 4)).reshape(seq_len, groups * GROUP * HEAD_DIM)
    return jnp.dot(head_outs, out_weight, preferred_element_type=jnp.float32).astype(jnp.bfloat16)
```

```python
import math

import jax
import jax.numpy as jnp
from jax import lax
from jax.experimental import pallas as pl
from jax.experimental.pallas import tpu as pltpu
from jax.sharding import PartitionSpec as P

HEAD_DIM = 128
GROUP = 8
LOW_SCORE = -1e30
FLOOR = -1e20
LANES = 4
LEVELS = 5
CHUNK = 512


def attention_kernel(ctx_ref, docs_ref, q_ref, *refs):
    count = LEVELS * LANES
    pieces, (out_ref, key_buf, value_buf, max_buf, sum_buf, sem) = refs[:count], refs[count:]
    rows = q_ref.shape[0]
    ctx = ctx_ref[0]
    lane = lax.rem(ctx, LANES)
    window = (ctx - lane - (LEVELS - 1) * LANES) * rows
    copies = []
    for index, piece in enumerate(pieces):
        back, flip = index // LANES, index % LANES
        slot = (LEVELS - 1 - back) * LANES + lax.bitwise_xor(lane, flip)
        at = pl.ds(pl.multiple_of(slot * rows, rows), rows)
        copies.append(pltpu.make_async_copy(piece.at[:, :HEAD_DIM], key_buf.at[at], sem.at[2 * index]))
        copies.append(pltpu.make_async_copy(piece.at[:, HEAD_DIM:], value_buf.at[at, :HEAD_DIM], sem.at[2 * index + 1]))
    for copy in copies:
        copy.start()
    first_row = ctx * rows
    row_pos = first_row + lax.broadcasted_iota(jnp.int32, (rows, 1), 0)
    row_low = jnp.zeros((rows, 1), jnp.int32)
    first_low, last_low, end = jnp.int32(0), jnp.int32(0), jnp.int32(0)
    for doc in range(docs_ref.shape[0]):
        end = end + docs_ref[doc]
        row_low = jnp.where(end <= row_pos, end, row_low)
        first_low = jnp.where(end <= first_row, end, first_low)
        last_low = jnp.where(end <= first_row + rows - 1, end, last_low)
    value_buf[:, HEAD_DIM:] = jnp.ones((value_buf.shape[0], HEAD_DIM), jnp.bfloat16)
    max_buf[...] = jnp.full(max_buf.shape, FLOOR, jnp.float32)
    sum_buf[...] = jnp.zeros(sum_buf.shape, jnp.float32)
    for copy in copies:
        copy.wait()
    log_scale = math.log2(math.e) / math.sqrt(HEAD_DIM)

    def one_head(head, begin, key_pos_begin, masked):
        columns = pl.ds(pl.multiple_of(head * HEAD_DIM, HEAD_DIM), HEAD_DIM)
        scores = lax.dot_general(
            q_ref[:, columns],
            key_buf[pl.ds(begin, CHUNK), :],
            (((1,), (1,)), ((), ())),
            preferred_element_type=jnp.float32,
        )
        scores = scores * log_scale
        if masked:
            key_pos = key_pos_begin + lax.broadcasted_iota(jnp.int32, (1, CHUNK), 1)
            allowed = (key_pos <= row_pos) & (key_pos >= row_low)
            scores = jnp.where(allowed, scores, LOW_SCORE)
        old_max = max_buf[head]
        new_max = jnp.maximum(old_max, jnp.max(scores, axis=1, keepdims=True))
        probs = jnp.exp2(scores - new_max[:, :1]).astype(jnp.bfloat16)
        shrink = jnp.exp2(old_max - new_max)
        added = jnp.dot(probs, value_buf[pl.ds(begin, CHUNK), :], preferred_element_type=jnp.float32)
        sum_buf[head] = sum_buf[head] * jnp.concatenate([shrink, shrink], axis=1) + added
        max_buf[head] = new_max

    def one_chunk(chunk, carry):
        begin = pl.multiple_of(chunk * CHUNK, CHUNK)
        key_pos_begin = window + begin
        free = (key_pos_begin >= last_low) & (key_pos_begin + CHUNK - 1 <= first_row)

        @pl.when(free)
        def _():
            for head in range(GROUP):
                one_head(head, begin, key_pos_begin, False)

        @pl.when(jnp.logical_not(free))
        def _():
            for head in range(GROUP):
                one_head(head, begin, key_pos_begin, True)

        return carry

    lax.fori_loop((first_low - window) // CHUNK, (first_row + rows - 1 - window) // CHUNK + 1, one_chunk, 0)
    for head in range(GROUP):
        total = sum_buf[head]
        out_ref[:, head * HEAD_DIM : (head + 1) * HEAD_DIM] = (
            total[:, :HEAD_DIM] / total[:, HEAD_DIM:]
        ).astype(jnp.bfloat16)


def attention(ctx, doc_lengths, queries, pieces):
    rows = queries.shape[0]
    held = LEVELS * LANES * rows
    smem, vmem, anywhere = (
        pl.BlockSpec(memory_space=pltpu.SMEM),
        pl.BlockSpec(memory_space=pltpu.VMEM),
        pl.BlockSpec(memory_space=pl.ANY),
    )
    return pl.pallas_call(
        attention_kernel,
        out_shape=jax.ShapeDtypeStruct(queries.shape, jnp.bfloat16),
        in_specs=[smem, smem, vmem] + [anywhere] * len(pieces),
        out_specs=vmem,
        scratch_shapes=[
            pltpu.VMEM((held, HEAD_DIM), jnp.bfloat16),
            pltpu.VMEM((held, 2 * HEAD_DIM), jnp.bfloat16),
            pltpu.VMEM((GROUP, rows, HEAD_DIM), jnp.float32),
            pltpu.VMEM((GROUP, rows, 2 * HEAD_DIM), jnp.float32),
            pltpu.SemaphoreType.DMA((2 * len(pieces),)),
        ],
        compiler_params=pltpu.CompilerParams(vmem_limit_bytes=40 * 1024 * 1024),
        cost_estimate=pl.CostEstimate(flops=5 * 10**9, bytes_accessed=4 * 10**6, transcendentals=8 * 10**6),
        name="attention",
    )(ctx, doc_lengths, queries, *pieces)


def turned(value, axis, steps):
    size = lax.axis_size(axis)
    return lax.ppermute(value, axis, [(source, (source + steps) % size) for source in range(size)])


def swapped(value, axis, flip):
    return lax.ppermute(value, axis, [(source, source ^ flip) for source in range(lax.axis_size(axis))])


def local(queries, keys, values, doc_lengths, out_weight):
    rows = queries.shape[0]
    ctx = lax.axis_index("ctx")
    me = lax.axis_index("head")
    own = jnp.concatenate([keys, values], axis=1)
    one_back = turned(own, "ctx", LANES)
    two_ahead = turned(own, "ctx", -2 * LANES)
    two_back = turned(one_back, "ctx", LANES)
    four_back = turned(two_ahead, "ctx", -2 * LANES)
    three_back = turned(two_back, "ctx", LANES)
    pieces = []
    for level in (own, one_back, two_back, three_back, four_back):
        across = swapped(level, "ctx", 2)
        pieces += [level, swapped(level, "ctx", 1), across, swapped(across, "ctx", 1)]
    attended = attention(ctx.reshape(1), doc_lengths, queries, pieces)
    below = turned(attended, "head", 2)
    above = turned(attended, "head", -2)
    beside = swapped(attended, "head", 1)
    half = rows // 2
    far_top = turned(below[:half], "head", 2)
    far_bottom = turned(above[half:], "head", -2)
    below_beside = turned(beside, "head", 2)
    above_beside = turned(beside, "head", -2)
    far_beside_top = swapped(far_top, "head", 1)
    far_beside_bottom = swapped(far_bottom, "head", 1)
    depth = queries.shape[1]
    count = lax.axis_size("head")

    def term(piece, steps, flip):
        source = lax.bitwise_xor((me + 2 * steps) % count, flip)
        return jnp.dot(
            piece,
            lax.dynamic_slice_in_dim(out_weight, source * depth, depth, 0),
            preferred_element_type=jnp.float32,
        )

    total = term(attended, 0, 0) + term(below, -1, 0) + term(above, 1, 0) + term(beside, 0, 1)
    total = total + term(jnp.concatenate([far_top, far_bottom]), 2, 0)
    total = total + term(below_beside, -1, 1) + term(above_beside, 1, 1)
    total = total + term(jnp.concatenate([far_beside_top, far_beside_bottom]), 2, 1)
    return total.astype(jnp.bfloat16)


def solution(mesh):
    placed = (P("ctx", "head"), P("ctx", "head"), P("ctx", "head"), P(), P(None, "head"))
    return jax.shard_map(
        local, mesh=mesh, in_specs=placed, out_specs=P("ctx", "head"), check_vma=False
    )
```

```python
import math

import jax
import jax.numpy as jnp
from jax import lax
from jax.experimental import pallas as pl
from jax.experimental.pallas import tpu as pltpu
from jax.sharding import PartitionSpec as P

HEAD_DIM = 128
GROUP = 8
LOW_SCORE = -1e30
FLOOR = -1e20
LANES = 4
LEVELS = 5
REACH = 16
STEP = 4


def attention_kernel(ctx_ref, docs_ref, q_ref, *refs):
    count = LEVELS * LANES
    pieces, (out_ref, key_buf, value_buf, max_buf, sum_buf, sems) = refs[:count], refs[count:]
    rows = q_ref.shape[0]
    ctx = ctx_ref[0]
    lane = lax.rem(ctx, LANES)
    newest = LEVELS * LANES - 1
    copies = []
    for index, piece in enumerate(pieces):
        back, flip = index // LANES, index % LANES
        behind = back * LANES + lane - lax.bitwise_xor(lane, flip)
        at = pl.ds(pl.multiple_of((newest - behind) * rows, rows), rows)
        copies.append(pltpu.make_async_copy(piece.at[:, :HEAD_DIM], key_buf.at[at], sems.at[2 * index]))
        copies.append(
            pltpu.make_async_copy(piece.at[:, HEAD_DIM:], value_buf.at[at, :HEAD_DIM], sems.at[2 * index + 1])
        )
    for copy in copies:
        copy.start()
    first_row = ctx * rows
    row_pos = first_row + lax.broadcasted_iota(jnp.int32, (rows, 1), 0)
    row_low = jnp.zeros((rows, 1), jnp.int32)
    first_low, last_low, end = jnp.int32(0), jnp.int32(0), jnp.int32(0)
    for doc in range(docs_ref.shape[0]):
        end = end + docs_ref[doc]
        row_low = jnp.where(end <= row_pos, end, row_low)
        first_low = jnp.where(end <= first_row, end, first_low)
        last_low = jnp.where(end <= first_row + rows - 1, end, last_low)
    value_buf[:, HEAD_DIM:] = jnp.ones((value_buf.shape[0], HEAD_DIM), jnp.bfloat16)
    max_buf[...] = jnp.full(max_buf.shape, FLOOR, jnp.float32)
    sum_buf[...] = jnp.zeros(sum_buf.shape, jnp.float32)
    for copy in copies:
        copy.wait()
    log_scale = math.log2(math.e) / math.sqrt(HEAD_DIM)

    def one_step(begin, size, masked):
        key_pos = first_row + begin - newest * rows + lax.broadcasted_iota(jnp.int32, (1, size), 1)
        held = pl.ds(begin, size)

        def scores_of(head):
            scores = lax.dot_general(
                q_ref[:, head * HEAD_DIM : (head + 1) * HEAD_DIM],
                key_buf[held, :],
                (((1,), (1,)), ((), ())),
                preferred_element_type=jnp.float32,
            )
            scores = scores * log_scale
            if masked:
                scores = jnp.where((key_pos <= row_pos) & (key_pos >= row_low), scores, LOW_SCORE)
            return scores

        scores = scores_of(0)
        for head in range(GROUP):
            following = scores_of(head + 1) if head + 1 < GROUP else None
            old_max = max_buf[head]
            new_max = jnp.maximum(old_max, jnp.max(scores, axis=1, keepdims=True))
            probs = jnp.exp2(scores - new_max[:, :1]).astype(jnp.bfloat16)
            shrink = jnp.exp2(old_max - new_max)
            added = jnp.dot(probs, value_buf[held, :], preferred_element_type=jnp.float32)
            sum_buf[head] = sum_buf[head] * jnp.concatenate([shrink, shrink], axis=1) + added
            max_buf[head] = new_max
            scores = following

    step_keys = STEP * rows
    one_step((newest + 1 - STEP) * rows, step_keys, True)

    def earlier_step(step, carry):
        begin = pl.multiple_of((newest + 1 - STEP) * rows - step * step_keys, rows)
        free = first_row + begin - newest * rows >= last_low
        pl.when(free)(lambda: one_step(begin, step_keys, False))
        pl.when(jnp.logical_not(free))(lambda: one_step(begin, step_keys, True))
        return carry

    reach = jnp.maximum(first_row - first_low, 0)
    own_step = (STEP - 1) * rows
    steps = jnp.minimum((reach - own_step + step_keys - 1) // step_keys, REACH // STEP - 1)
    lax.fori_loop(1, steps + 1, earlier_step, 0)
    pl.when(reach > (REACH - 1) * rows)(lambda: one_step((newest - REACH) * rows, rows, True))
    for head in range(GROUP):
        total = sum_buf[head]
        out_ref[:, head * HEAD_DIM : (head + 1) * HEAD_DIM] = (
            total[:, :HEAD_DIM] / total[:, HEAD_DIM:]
        ).astype(jnp.bfloat16)


def attention(ctx, doc_lengths, queries, pieces):
    rows = queries.shape[0]
    held = (LEVELS * LANES + LANES - 1) * rows
    smem, vmem, anywhere = (
        pl.BlockSpec(memory_space=pltpu.SMEM),
        pl.BlockSpec(memory_space=pltpu.VMEM),
        pl.BlockSpec(memory_space=pl.ANY),
    )
    return pl.pallas_call(
        attention_kernel,
        out_shape=jax.ShapeDtypeStruct(queries.shape, jnp.bfloat16),
        in_specs=[smem, smem, vmem] + [anywhere] * len(pieces),
        out_specs=vmem,
        scratch_shapes=[
            pltpu.VMEM((held, HEAD_DIM), jnp.bfloat16),
            pltpu.VMEM((held, 2 * HEAD_DIM), jnp.bfloat16),
            pltpu.VMEM((GROUP, rows, HEAD_DIM), jnp.float32),
            pltpu.VMEM((GROUP, rows, 2 * HEAD_DIM), jnp.float32),
            pltpu.SemaphoreType.DMA((2 * len(pieces),)),
        ],
        compiler_params=pltpu.CompilerParams(vmem_limit_bytes=40 * 1024 * 1024),
        cost_estimate=pl.CostEstimate(flops=5 * 10**9, bytes_accessed=4 * 10**6, transcendentals=8 * 10**6),
        name="attention",
    )(ctx, doc_lengths, queries, *pieces)


def turned(value, axis, steps):
    size = lax.axis_size(axis)
    return lax.ppermute(value, axis, [(source, (source + steps) % size) for source in range(size)])


def swapped(value, axis, flip):
    return lax.ppermute(value, axis, [(source, source ^ flip) for source in range(lax.axis_size(axis))])


def local(queries, keys, values, doc_lengths, out_weight):
    rows = queries.shape[0]
    ctx = lax.axis_index("ctx")
    me = lax.axis_index("head")
    own = jnp.concatenate([keys, values], axis=1)
    one_back = turned(own, "ctx", LANES)
    two_ahead = turned(own, "ctx", -2 * LANES)
    two_back = turned(one_back, "ctx", LANES)
    four_back = turned(two_ahead, "ctx", -2 * LANES)
    three_back = turned(two_back, "ctx", LANES)
    pieces = []
    for level in (own, one_back, two_back, three_back, four_back):
        across = swapped(level, "ctx", 2)
        pieces += [level, swapped(level, "ctx", 1), across, swapped(across, "ctx", 1)]
    attended = attention(ctx.reshape(1), doc_lengths, queries, pieces)
    below = turned(attended, "head", 2)
    above = turned(attended, "head", -2)
    beside = swapped(attended, "head", 1)
    half = rows // 2
    far_top = turned(below[:half], "head", 2)
    far_bottom = turned(above[half:], "head", -2)
    below_beside = turned(beside, "head", 2)
    above_beside = turned(beside, "head", -2)
    far_beside_top = swapped(far_top, "head", 1)
    far_beside_bottom = swapped(far_bottom, "head", 1)
    depth = queries.shape[1]
    count = lax.axis_size("head")

    def term(piece, steps, flip):
        source = lax.bitwise_xor((me + 2 * steps) % count, flip)
        return jnp.dot(
            piece,
            lax.dynamic_slice_in_dim(out_weight, source * depth, depth, 0),
            preferred_element_type=jnp.float32,
        )

    total = term(attended, 0, 0) + term(below, -1, 0) + term(above, 1, 0) + term(beside, 0, 1)
    total = total + term(jnp.concatenate([far_top, far_bottom]), 2, 0)
    total = total + term(below_beside, -1, 1) + term(above_beside, 1, 1)
    total = total + term(jnp.concatenate([far_beside_top, far_beside_bottom]), 2, 1)
    return total.astype(jnp.bfloat16)


def solution(mesh):
    placed = (P("ctx", "head"), P("ctx", "head"), P("ctx", "head"), P(), P(None, "head"))
    return jax.shard_map(
        local, mesh=mesh, in_specs=placed, out_specs=P("ctx", "head"), check_vma=False
    )
```

```python
import math

import jax
import jax.numpy as jnp
from jax import lax
from jax.experimental import pallas as pl
from jax.experimental.pallas import tpu as pltpu
from jax.sharding import PartitionSpec as P

HEAD_DIM = 128
GROUP = 8
LOW_SCORE = -1e30
FLOOR = -1e20
LANES = 4
LEVELS = 5
REACH = 16
STEP = 4


def attention_kernel(meta_ref, q_ref, *refs):
    count = LEVELS * LANES
    pieces, (out_ref, key_buf, value_buf, max_buf, sum_buf, sems) = refs[:count], refs[count:]
    rows = q_ref.shape[0]
    ctx = meta_ref[0]
    lane = lax.rem(ctx, LANES)
    newest = LEVELS * LANES - 1
    copies = []
    for index, piece in enumerate(pieces):
        back, flip = index // LANES, index % LANES
        behind = back * LANES + lane - lax.bitwise_xor(lane, flip)
        at = pl.ds(pl.multiple_of((newest - behind) * rows, rows), rows)
        copies.append(pltpu.make_async_copy(piece.at[:, :HEAD_DIM], key_buf.at[at], sems.at[2 * index]))
        copies.append(
            pltpu.make_async_copy(piece.at[:, HEAD_DIM:], value_buf.at[at, :HEAD_DIM], sems.at[2 * index + 1])
        )
    for copy in copies:
        copy.start()
    first_row = ctx * rows
    row_pos = first_row + lax.broadcasted_iota(jnp.int32, (rows, 1), 0)
    row_low = jnp.zeros((rows, 1), jnp.int32)
    first_low, last_low, end = jnp.int32(0), jnp.int32(0), jnp.int32(0)
    for entry in range(1, meta_ref.shape[0]):
        end = end + meta_ref[entry]
        row_low = jnp.where(end <= row_pos, end, row_low)
        first_low = jnp.where(end <= first_row, end, first_low)
        last_low = jnp.where(end <= first_row + rows - 1, end, last_low)
    value_buf[:, HEAD_DIM:] = jnp.ones((value_buf.shape[0], HEAD_DIM), jnp.bfloat16)
    max_buf[...] = jnp.full(max_buf.shape, FLOOR, jnp.float32)
    sum_buf[...] = jnp.zeros(sum_buf.shape, jnp.float32)
    for copy in copies:
        copy.wait()
    log_scale = math.log2(math.e) / math.sqrt(HEAD_DIM)

    def one_step(begin, size, masked):
        key_pos = first_row + begin - newest * rows + lax.broadcasted_iota(jnp.int32, (1, size), 1)
        held = pl.ds(begin, size)

        def scores_of(head):
            scores = lax.dot_general(
                q_ref[:, head * HEAD_DIM : (head + 1) * HEAD_DIM],
                key_buf[held, :],
                (((1,), (1,)), ((), ())),
                preferred_element_type=jnp.float32,
            )
            scores = scores * log_scale
            if masked:
                scores = jnp.where((key_pos <= row_pos) & (key_pos >= row_low), scores, LOW_SCORE)
            return scores

        scores = scores_of(0)
        for head in range(GROUP):
            following = scores_of(head + 1) if head + 1 < GROUP else None
            old_max = max_buf[head]
            new_max = jnp.maximum(old_max, jnp.max(scores, axis=1, keepdims=True))
            probs = jnp.exp2(scores - new_max[:, :1]).astype(jnp.bfloat16)
            shrink = jnp.exp2(old_max - new_max)
            added = jnp.dot(probs, value_buf[held, :], preferred_element_type=jnp.float32)
            sum_buf[head] = sum_buf[head] * jnp.concatenate([shrink, shrink], axis=1) + added
            max_buf[head] = new_max
            scores = following

    step_keys = STEP * rows
    one_step((newest + 1 - STEP) * rows, step_keys, True)

    def earlier_step(step, carry):
        begin = pl.multiple_of((newest + 1 - STEP) * rows - step * step_keys, rows)
        free = first_row + begin - newest * rows >= last_low
        pl.when(free)(lambda: one_step(begin, step_keys, False))
        pl.when(jnp.logical_not(free))(lambda: one_step(begin, step_keys, True))
        return carry

    reach = jnp.maximum(first_row - first_low, 0)
    own_step = (STEP - 1) * rows
    steps = jnp.minimum((reach - own_step + step_keys - 1) // step_keys, REACH // STEP - 1)
    lax.fori_loop(1, steps + 1, earlier_step, 0)
    pl.when(reach > (REACH - 1) * rows)(lambda: one_step((newest - REACH) * rows, rows, True))
    for head in range(GROUP):
        total = sum_buf[head]
        out_ref[:, head * HEAD_DIM : (head + 1) * HEAD_DIM] = (
            total[:, :HEAD_DIM] / total[:, HEAD_DIM:]
        ).astype(jnp.bfloat16)


def attention(ctx, doc_lengths, queries, pieces):
    meta = jnp.concatenate([ctx, doc_lengths])
    rows = queries.shape[0]
    held = (LEVELS * LANES + LANES - 1) * rows
    smem, vmem, anywhere = (
        pl.BlockSpec(memory_space=pltpu.SMEM),
        pl.BlockSpec(memory_space=pltpu.VMEM),
        pl.BlockSpec(memory_space=pl.ANY),
    )
    return pl.pallas_call(
        attention_kernel,
        out_shape=jax.ShapeDtypeStruct(queries.shape, jnp.bfloat16),
        in_specs=[smem, vmem] + [anywhere] * len(pieces),
        out_specs=vmem,
        scratch_shapes=[
            pltpu.VMEM((held, HEAD_DIM), jnp.bfloat16),
            pltpu.VMEM((held, 2 * HEAD_DIM), jnp.bfloat16),
            pltpu.VMEM((GROUP, rows, HEAD_DIM), jnp.float32),
            pltpu.VMEM((GROUP, rows, 2 * HEAD_DIM), jnp.float32),
            pltpu.SemaphoreType.DMA((2 * len(pieces),)),
        ],
        compiler_params=pltpu.CompilerParams(vmem_limit_bytes=40 * 1024 * 1024),
        cost_estimate=pl.CostEstimate(flops=5 * 10**9, bytes_accessed=4 * 10**6, transcendentals=8 * 10**6),
        name="attention",
    )(meta, queries, *pieces)


def join_kernel(top_ref, bottom_ref, joined_ref):
    half = top_ref.shape[0]
    joined_ref[:half] = top_ref[...]
    joined_ref[half:] = bottom_ref[...]


def joined(top, bottom):
    half, depth = top.shape
    in_vmem = pl.BlockSpec(memory_space=pltpu.VMEM)
    return pl.pallas_call(
        join_kernel,
        out_shape=jax.ShapeDtypeStruct((2 * half, depth), top.dtype),
        in_specs=[in_vmem, in_vmem],
        out_specs=in_vmem,
        compiler_params=pltpu.CompilerParams(vmem_limit_bytes=40 * 1024 * 1024),
        cost_estimate=pl.CostEstimate(flops=0, bytes_accessed=2**20, transcendentals=0),
        name="joined",
    )(top, bottom)


def turned(value, axis, steps):
    size = lax.axis_size(axis)
    return lax.ppermute(value, axis, [(source, (source + steps) % size) for source in range(size)])


def swapped(value, axis, flip):
    return lax.ppermute(value, axis, [(source, source ^ flip) for source in range(lax.axis_size(axis))])


def local(queries, keys, values, doc_lengths, out_weight):
    rows = queries.shape[0]
    ctx = lax.axis_index("ctx")
    me = lax.axis_index("head")
    own = jnp.concatenate([keys, values], axis=1)
    one_back = turned(own, "ctx", LANES)
    two_ahead = turned(own, "ctx", -2 * LANES)
    two_back = turned(one_back, "ctx", LANES)
    four_back = turned(two_ahead, "ctx", -2 * LANES)
    three_back = turned(two_back, "ctx", LANES)
    pieces = []
    for level in (own, one_back, two_back, three_back, four_back):
        across = swapped(level, "ctx", 2)
        pieces += [level, swapped(level, "ctx", 1), across, swapped(across, "ctx", 1)]
    attended = attention(ctx.reshape(1), doc_lengths, queries, pieces)
    below = turned(attended, "head", 2)
    above = turned(attended, "head", -2)
    beside = swapped(attended, "head", 1)
    half = rows // 2
    far_top = turned(below[:half], "head", 2)
    far_bottom = turned(above[half:], "head", -2)
    far = joined(far_top, far_bottom)
    below_beside = turned(beside, "head", 2)
    above_beside = turned(beside, "head", -2)
    far_beside = swapped(far, "head", 1)
    depth = queries.shape[1]
    count = lax.axis_size("head")

    def term(piece, steps, flip):
        source = lax.bitwise_xor((me + 2 * steps) % count, flip)
        return jnp.dot(
            piece,
            lax.dynamic_slice_in_dim(out_weight, source * depth, depth, 0),
            preferred_element_type=jnp.float32,
        )

    total = term(attended, 0, 0) + term(below, -1, 0) + term(above, 1, 0) + term(beside, 0, 1)
    total = total + term(far, 2, 0)
    total = total + term(below_beside, -1, 1) + term(above_beside, 1, 1)
    total = total + term(far_beside, 2, 1)
    return total.astype(jnp.bfloat16)


def solution(mesh):
    placed = (P("ctx", "head"), P("ctx", "head"), P("ctx", "head"), P(), P(None, "head"))
    return jax.shard_map(
        local, mesh=mesh, in_specs=placed, out_specs=P("ctx", "head"), check_vma=False
    )
```

```python
import math

import jax
import jax.numpy as jnp
from jax import lax
from jax.experimental import pallas as pl
from jax.experimental.pallas import tpu as pltpu
from jax.sharding import PartitionSpec as P

HEAD_DIM = 128
GROUP = 8
LOW_SCORE = -1e30
FLOOR = -1e20
LANES = 4
LEVELS = 5
REACH = 16
STEP = 4


def attention_kernel(meta_ref, q_ref, *refs):
    count = LEVELS * LANES
    pieces, (out_ref, key_buf, value_buf, max_buf, sum_buf, sems) = refs[:count], refs[count:]
    rows = q_ref.shape[0]
    ctx = meta_ref[0]
    lane = lax.rem(ctx, LANES)
    newest = LEVELS * LANES - 1
    copies = []
    for index, piece in enumerate(pieces):
        back, flip = index // LANES, index % LANES
        behind = back * LANES + lane - lax.bitwise_xor(lane, flip)
        at = pl.ds(pl.multiple_of((newest - behind) * rows, rows), rows)
        copies.append(pltpu.make_async_copy(piece.at[:, :HEAD_DIM], key_buf.at[at], sems.at[2 * index]))
        copies.append(
            pltpu.make_async_copy(piece.at[:, HEAD_DIM:], value_buf.at[at, :HEAD_DIM], sems.at[2 * index + 1])
        )
    for copy in copies:
        copy.start()
    first_row = ctx * rows
    row_pos = first_row + lax.broadcasted_iota(jnp.int32, (rows, 1), 0)
    row_low = jnp.zeros((rows, 1), jnp.int32)
    first_low, last_low, end = jnp.int32(0), jnp.int32(0), jnp.int32(0)
    for entry in range(1, meta_ref.shape[0]):
        end = end + meta_ref[entry]
        row_low = jnp.where(end <= row_pos, end, row_low)
        first_low = jnp.where(end <= first_row, end, first_low)
        last_low = jnp.where(end <= first_row + rows - 1, end, last_low)
    value_buf[:, HEAD_DIM:] = jnp.ones((value_buf.shape[0], HEAD_DIM), jnp.bfloat16)
    max_buf[...] = jnp.full(max_buf.shape, FLOOR, jnp.float32)
    sum_buf[...] = jnp.zeros(sum_buf.shape, jnp.float32)
    for copy in copies:
        copy.wait()
    log_scale = math.log2(math.e) / math.sqrt(HEAD_DIM)

    def one_step(begin, size, masked):
        key_pos = first_row + begin - newest * rows + lax.broadcasted_iota(jnp.int32, (1, size), 1)
        held = pl.ds(begin, size)

        def scores_of(head):
            scores = lax.dot_general(
                q_ref[:, head * HEAD_DIM : (head + 1) * HEAD_DIM],
                key_buf[held, :],
                (((1,), (1,)), ((), ())),
                preferred_element_type=jnp.float32,
            )
            scores = scores * log_scale
            if masked:
                scores = jnp.where((key_pos <= row_pos) & (key_pos >= row_low), scores, LOW_SCORE)
            return scores

        scores = scores_of(0)
        for head in range(GROUP):
            following = scores_of(head + 1) if head + 1 < GROUP else None
            old_max = max_buf[head]
            new_max = jnp.maximum(old_max, jnp.max(scores, axis=1, keepdims=True))
            probs = jnp.exp2(scores - new_max[:, :1]).astype(jnp.bfloat16)
            shrink = jnp.exp2(old_max - new_max)
            added = jnp.dot(probs, value_buf[held, :], preferred_element_type=jnp.float32)
            sum_buf[head] = sum_buf[head] * jnp.concatenate([shrink, shrink], axis=1) + added
            max_buf[head] = new_max
            scores = following

    step_keys = STEP * rows
    one_step((newest + 1 - STEP) * rows, step_keys, True)

    def earlier_step(step, carry):
        begin = pl.multiple_of((newest + 1 - STEP) * rows - step * step_keys, rows)
        free = first_row + begin - newest * rows >= last_low
        pl.when(free)(lambda: one_step(begin, step_keys, False))
        pl.when(jnp.logical_not(free))(lambda: one_step(begin, step_keys, True))
        return carry

    reach = jnp.maximum(first_row - first_low, 0)
    own_step = (STEP - 1) * rows
    steps = jnp.minimum((reach - own_step + step_keys - 1) // step_keys, REACH // STEP - 1)
    lax.fori_loop(1, steps + 1, earlier_step, 0)
    pl.when(reach > (REACH - 1) * rows)(lambda: one_step((newest - REACH) * rows, rows, True))
    for head in range(GROUP):
        total = sum_buf[head]
        out_ref[:, head * HEAD_DIM : (head + 1) * HEAD_DIM] = (
            total[:, :HEAD_DIM] / total[:, HEAD_DIM:]
        ).astype(jnp.bfloat16)


def attention(ctx, doc_lengths, queries, pieces):
    meta = jnp.concatenate([ctx, doc_lengths])
    rows = queries.shape[0]
    held = (LEVELS * LANES + LANES - 1) * rows
    smem, vmem, anywhere = (
        pl.BlockSpec(memory_space=pltpu.SMEM),
        pl.BlockSpec(memory_space=pltpu.VMEM),
        pl.BlockSpec(memory_space=pl.ANY),
    )
    return pl.pallas_call(
        attention_kernel,
        out_shape=jax.ShapeDtypeStruct(queries.shape, jnp.bfloat16),
        in_specs=[smem, vmem] + [anywhere] * len(pieces),
        out_specs=vmem,
        scratch_shapes=[
            pltpu.VMEM((held, HEAD_DIM), jnp.bfloat16),
            pltpu.VMEM((held, 2 * HEAD_DIM), jnp.bfloat16),
            pltpu.VMEM((GROUP, rows, HEAD_DIM), jnp.float32),
            pltpu.VMEM((GROUP, rows, 2 * HEAD_DIM), jnp.float32),
            pltpu.SemaphoreType.DMA((2 * len(pieces),)),
        ],
        compiler_params=pltpu.CompilerParams(vmem_limit_bytes=40 * 1024 * 1024),
        cost_estimate=pl.CostEstimate(flops=5 * 10**9, bytes_accessed=4 * 10**6, transcendentals=8 * 10**6),
        name="attention",
    )(meta, queries, *pieces)


def join_kernel(top_ref, bottom_ref, below_ref, above_ref, joined_ref, below_out_ref, above_out_ref):
    half = top_ref.shape[0]
    joined_ref[:half] = top_ref[...]
    joined_ref[half:] = bottom_ref[...]


def joined_before(top, bottom, below, above):
    in_vmem, anywhere = pl.BlockSpec(memory_space=pltpu.VMEM), pl.BlockSpec(memory_space=pl.ANY)
    return pl.pallas_call(
        join_kernel,
        out_shape=[jax.ShapeDtypeStruct(below.shape, below.dtype)] * 3,
        in_specs=[in_vmem, in_vmem, anywhere, anywhere],
        out_specs=[in_vmem, anywhere, anywhere],
        input_output_aliases={2: 1, 3: 2},
        compiler_params=pltpu.CompilerParams(vmem_limit_bytes=40 * 1024 * 1024),
        cost_estimate=pl.CostEstimate(flops=0, bytes_accessed=2**20, transcendentals=0),
        name="joined_before",
    )(top, bottom, below, above)


def turned(value, axis, steps):
    size = lax.axis_size(axis)
    return lax.ppermute(value, axis, [(source, (source + steps) % size) for source in range(size)])


def swapped(value, axis, flip):
    return lax.ppermute(value, axis, [(source, source ^ flip) for source in range(lax.axis_size(axis))])


def local(queries, keys, values, doc_lengths, out_weight):
    rows = queries.shape[0]
    ctx = lax.axis_index("ctx")
    me = lax.axis_index("head")
    own = jnp.concatenate([keys, values], axis=1)
    one_back = turned(own, "ctx", LANES)
    two_ahead = turned(own, "ctx", -2 * LANES)
    two_back = turned(one_back, "ctx", LANES)
    four_back = turned(two_ahead, "ctx", -2 * LANES)
    three_back = turned(two_back, "ctx", LANES)
    pieces = []
    for level in (own, one_back, two_back, three_back, four_back):
        across = swapped(level, "ctx", 2)
        pieces += [level, swapped(level, "ctx", 1), across, swapped(across, "ctx", 1)]
    attended = attention(ctx.reshape(1), doc_lengths, queries, pieces)
    below = turned(attended, "head", 2)
    above = turned(attended, "head", -2)
    beside = swapped(attended, "head", 1)
    half = rows // 2
    far_top = turned(below[:half], "head", 2)
    far_bottom = turned(above[half:], "head", -2)
    far, below, above = joined_before(far_top, far_bottom, below, above)
    below_beside = turned(beside, "head", 2)
    above_beside = turned(beside, "head", -2)
    far_beside = swapped(far, "head", 1)
    depth = queries.shape[1]
    count = lax.axis_size("head")

    def term(piece, steps, flip):
        source = lax.bitwise_xor((me + 2 * steps) % count, flip)
        return jnp.dot(
            piece,
            lax.dynamic_slice_in_dim(out_weight, source * depth, depth, 0),
            preferred_element_type=jnp.float32,
        )

    total = term(attended, 0, 0) + term(below, -1, 0) + term(above, 1, 0) + term(beside, 0, 1)
    total = total + term(far, 2, 0)
    total = total + term(below_beside, -1, 1) + term(above_beside, 1, 1)
    total = total + term(far_beside, 2, 1)
    return total.astype(jnp.bfloat16)


def solution(mesh):
    placed = (P("ctx", "head"), P("ctx", "head"), P("ctx", "head"), P(), P(None, "head"))
    return jax.shard_map(
        local, mesh=mesh, in_specs=placed, out_specs=P("ctx", "head"), check_vma=False
    )
```
